32 devices in a mesh: groups: 2 (over x), space: 16 (over z, y, core).
Axes of the slice: x: 2, y: 2, z: 4, core: 2. Of those that a mesh axis runs over, the one named last changes fastest.
Arguments:
- snapshots: bfloat16 [256, 128, 128], P(('groups', 'space')), parts along dimension 0, may hold values from -6 to 6
- weights: bfloat16 [256, 128, 1024], P(('groups', 'space')), parts along dimension 0, may hold values from -6 to 6
- neighbours: int32 [256, 8], P(('groups', 'space')), parts along dimension 0, may hold values from 0 to 127, as said below
- time_of: int32 [256], P('groups'), parts along dimension 0, may hold values from 0 to 127, each once
Outputs:
- new_weights: float32 [256, 128, 1024], P(('groups', 'space')), parts along dimension 0
- cell_error: float32 [256, 128], P(('groups', 'space')), parts along dimension 0
The draws below stay inside these ranges and needn't reach their ends.
There are 2 independent parts, one for each index of `groups`. The reference program is written for one: setup_inputs(seed, part) draws one part's arguments, and reference() takes and returns one part's arrays. A program takes and returns all parts, laid end to end along the dimension named above; each array names one. Nothing has to cross between parts.
Inputs may be any that keep to these rules, and one draw needn't show every extreme that they name: `neighbours`: row g lists 8 groups in a drawn order: g itself, g - 4, g + 4, and 5 more within 4 groups of g, all counted cyclically modulo 128; entries may repeat. `time_of`: each time index appears once.
All inputs are finite; a program needn't handle non-finite values.
Results may differ from the reference program's by a relative error of at most 0.002.
Values may be sent and summed in bfloat16 or wider, within the bound.
A program may use at most 64 MiB of HBM per device.

```python
import jax
import jax.numpy as jnp
from jax import lax

B = 128
K = 8
HALO = 4
G = 128
T_SIZE = 128


def draw_neighbours(key, part):
    key_extra = jax.random.fold_in(key, 11)
    key_order = jax.random.fold_in(key, 23)
    extra = jax.random.randint(key_extra, (G, K - 3), -HALO, HALO + 1)
    fixed = jnp.broadcast_to(jnp.array([0, -HALO, HALO], dtype=jnp.int32), (G, 3))
    offsets = jnp.concatenate([fixed, extra.astype(jnp.int32)], axis=1)
    row_keys = jax.random.split(key_order, G)
    offsets = jax.vmap(lambda k, r: jax.random.permutation(k, r))(row_keys, offsets)
    return ((jnp.arange(G, dtype=jnp.int32)[:, None] + offsets) % G).astype(jnp.int32)


def shard_levels(own_key, shape, pieces, low, high):
    factor_of = 1.0
    for dim, shards_of in pieces:
        draws = jax.random.uniform(jax.random.fold_in(jax.random.fold_in(own_key, 6), dim), (shards_of,), jnp.float32, low / len(pieces), high / len(pieces))
        factor_of = factor_of * jnp.repeat(jnp.exp(draws), shape[dim] // shards_of).reshape((-1,) + (1,) * (len(shape) - 1 - dim))
    return factor_of


def centred(rng, extent, width, bound, cuts=(), held_as=jnp.bfloat16):
    drawn = jax.random.normal(rng, extent, jnp.float32) * width
    if len(cuts) > 0:
        drawn = shard_levels(rng, extent, cuts, -0.22, 0.18) * drawn
    return jnp.clip(drawn, min=-bound, max=bound).astype(held_as)


def setup_inputs(seed: int = 0, part: int = 0) -> dict:
    splits = jax.random.split(jax.random.key(seed), 5)
    part_keys = jax.random.split(jax.random.fold_in(splits[4], part), 5)
    snapshots = centred(part_keys[0], (T_SIZE, G, B), 1.0, 6.0, ((0, 16),))
    weights = centred(part_keys[1], (G, B, K * B), 1.0, 6.0, ((0, 16),))
    neighbours = draw_neighbours(jax.random.fold_in(jax.random.fold_in(splits[4], part), 71), part)
    time_of = jax.random.permutation(part_keys[3], T_SIZE).astype(jnp.int32)
    return dict(snapshots=snapshots, weights=weights, neighbours=neighbours, time_of=time_of)


def reference(snapshots, weights, neighbours, time_of):
    step_rate = 100.0
    order = jnp.argsort(time_of).astype(jnp.int32)
    ordered = snapshots[order]
    target = jnp.roll(ordered, -1, 0).astype(jnp.float32)
    scale = 1.0 / jnp.sqrt(jnp.float32(K * B))
    live = (jnp.arange(T_SIZE) < T_SIZE - 1).astype(jnp.float32)[:, None]

    def one_group(g):
        inputs = ordered[:, neighbours[g]].reshape(T_SIZE, K * B)
        block = weights[g]
        pred = jnp.dot(inputs, block.T, preferred_element_type=jnp.float32) * scale
        resid = ((pred - target[:, g]) * live).astype(jnp.bfloat16)
        grad = jnp.dot(resid.T, inputs, preferred_element_type=jnp.float32) * (2.0 * scale / (T_SIZE - 1))
        fresh = block.astype(jnp.float32) - step_rate * grad
        fresh_b = fresh.astype(jnp.bfloat16)
        after = (jnp.dot(inputs, fresh_b.T, preferred_element_type=jnp.float32) * scale - target[:, g]) * live
        return (fresh, lax.optimization_barrier(jnp.sum(after * after, axis=0)) / (T_SIZE - 1))
    new_weights, cell_error = lax.map(one_group, jnp.arange(G))
    return (new_weights, cell_error)
```

```python
import functools

import jax
import jax.numpy as jnp
from jax import lax
from jax.experimental import pallas as pl
from jax.experimental.pallas import tpu as pltpu
from jax.sharding import PartitionSpec as P

HALO = 4
MESH = pl.DeviceIdType.MESH


def gather_kernel(n, snaps, x, wide, flat, recv, send_sem, recv_sem):
    rows, groups, cells = snaps.shape
    g_dev = groups // n
    span = g_dev + 2 * HALO
    me = lax.axis_index("space")

    barrier = pltpu.get_barrier_semaphore()
    for i in range(1, n):
        pl.semaphore_signal(
            barrier, inc=1, device_id={"space": lax.rem(me + i, n)}, device_id_type=MESH
        )

    step = 16

    @pl.loop(0, groups // step)
    def _(b):
        first = pl.multiple_of(b * step, step)
        block = snaps[:, pl.ds(first, step), :].astype(jnp.float32)
        wide[...] = block.reshape(rows * step, cells)
        for q in range(step // 2):
            pair = jnp.concatenate(
                [wide[pl.ds(2 * q + h, rows, stride=step), :] for h in range(2)], axis=0
            )
            at = pl.multiple_of((first + HALO + 2 * q) * rows, 2 * rows)
            flat[pl.ds(at, 2 * rows), :] = pair.astype(jnp.bfloat16)

    edge = HALO * rows
    flat[:edge, :] = flat[groups * rows : groups * rows + edge, :]
    flat[(groups + HALO) * rows :, :] = flat[edge : 2 * edge, :]

    pl.semaphore_wait(barrier, n - 1)

    def copy(i):
        to = lax.rem(me + i, n)
        part = pl.ds(pl.multiple_of(to * (g_dev * rows), g_dev * rows), span * rows)
        return pltpu.make_async_remote_copy(
            src_ref=flat.at[part, :],
            dst_ref=recv.at[me],
            send_sem=send_sem.at[i],
            recv_sem=recv_sem.at[i],
            device_id={"space": to},
            device_id_type=MESH,
        )

    order = sorted(range(1, n), key=lambda i: -min(i, n - i))
    for i in order:
        copy(i).start()

    def place(src, block):
        at = pl.multiple_of(src * rows, rows)
        x[:, pl.ds(at, rows), :] = block.reshape(span, rows, cells)

    own = pl.ds(pl.multiple_of(me * (g_dev * rows), g_dev * rows), span * rows)
    place(me, flat[own, :].astype(jnp.float32))
    for i in reversed(order):
        copy(i).wait_recv()
        src = lax.rem(me + n - i, n)
        place(src, recv[src].astype(jnp.float32))
    for i in order:
        copy(i).wait_send()


def gathered(snaps, n):
    rows, groups, cells = snaps.shape
    g_dev = groups // n
    span = g_dev + 2 * HALO
    return pl.pallas_call(
        functools.partial(gather_kernel, n),
        out_shape=jax.ShapeDtypeStruct((span, rows * n, cells), jnp.float32),
        in_specs=[pl.BlockSpec(memory_space=pltpu.VMEM)],
        out_specs=pl.BlockSpec(memory_space=pltpu.VMEM),
        scratch_shapes=[
            pltpu.VMEM((rows * 16, cells), jnp.float32),
            pltpu.VMEM(((groups + 2 * HALO) * rows, cells), jnp.bfloat16),
            pltpu.VMEM((n, span * rows, cells), jnp.bfloat16),
            pltpu.SemaphoreType.DMA((n,)),
            pltpu.SemaphoreType.DMA((n,)),
        ],
        compiler_params=pltpu.CompilerParams(
            collective_id=0, has_side_effects=True, vmem_limit_bytes=40 * 2**20
        ),
        cost_estimate=pl.CostEstimate(
            flops=0, bytes_accessed=4 * span * rows * n * cells, transcendentals=0
        ),
    )(snaps)


def step_kernel(n, per, nb, x, times, weights, fresh_out, error_out, goal, inputs, xb):
    span, total, cells = x.shape
    g_dev = span - 2 * HALO
    width = g_dev * n
    depth = weights.shape[2]
    scale = 1.0 / (depth**0.5)
    step_rate = 100.0
    me = lax.axis_index("space")
    at = pl.program_id(0)
    tile = 128
    turns = total // tile

    def columns(b):
        row = times[:, pl.ds(pl.multiple_of(b * tile, tile), tile)]
        return jnp.transpose(jnp.broadcast_to(row, (tile, tile)))

    @pl.when(at == 0)
    def _():
        xb[...] = x[...].astype(jnp.bfloat16)

        def rows_of(b):
            after = columns(b) + 1.0
            for g in range(g_dev):
                def add(c, acc):
                    row = times[:, pl.ds(pl.multiple_of(c * tile, tile), tile)]
                    pick = (after == row).astype(jnp.bfloat16)
                    part = xb[HALO + g, pl.ds(pl.multiple_of(c * tile, tile), tile), :]
                    return acc + jnp.dot(pick, part, preferred_element_type=jnp.float32)

                acc = jnp.zeros((tile, cells), jnp.float32)
                acc = add(0, acc) if turns == 1 else lax.fori_loop(0, turns, add, acc)
                goal[g, pl.ds(pl.multiple_of(b * tile, tile), tile), :] = acc

        if turns == 1:
            rows_of(0)
        else:
            pl.loop(0, turns)(rows_of)

    for p in range(per):
        g = at * per + p
        for k in range(depth // cells):
            local = lax.rem(nb[g, k] - (me * g_dev + g) + HALO + width, width) + g
            inputs[p, :, k * cells : (k + 1) * cells] = xb[local]
        w = weights[p]

        def forward(b, matrix):
            part = pl.ds(pl.multiple_of(b * tile, tile), tile)
            out = lax.dot_general(
                inputs[p, part, :], matrix, (((1,), (1,)), ((), ())),
                preferred_element_type=jnp.float32,
            )
            live = (columns(b) != float(total - 1)).astype(jnp.float32)
            return (out * scale - goal[g, part, :]) * live

        def add_grad(b, acc):
            part = pl.ds(pl.multiple_of(b * tile, tile), tile)
            resid = forward(b, w).astype(jnp.bfloat16)
            return acc + lax.dot_general(
                resid, inputs[p, part, :], (((0,), (0,)), ((), ())),
                preferred_element_type=jnp.float32,
            )

        acc = jnp.zeros((cells, depth), jnp.float32)
        acc = add_grad(0, acc) if turns == 1 else lax.fori_loop(0, turns, add_grad, acc)
        fresh = w.astype(jnp.float32) - acc * (step_rate * 2.0 * scale / (total - 1))
        fresh_out[p] = fresh
        fresh_b = fresh.astype(jnp.bfloat16)

        def add_error(b, acc):
            out = forward(b, fresh_b)
            return acc + jnp.sum(out * out, axis=0, keepdims=True)

        acc = jnp.zeros((1, cells), jnp.float32)
        acc = add_error(0, acc) if turns == 1 else lax.fori_loop(0, turns, add_error, acc)
        error_out[pl.ds(g, 1), :] = acc * (1.0 / (total - 1))


def shards(snapshots, weights, neighbours, time_of):
    n = lax.axis_size("space")
    g_dev, cells, depth = weights.shape
    total = time_of.shape[0]
    span = g_dev + 2 * HALO
    x = gathered(snapshots, n)
    times = time_of.astype(jnp.float32).reshape(1, total)
    per = 2
    flops = 6 * g_dev * total * cells * depth
    return pl.pallas_call(
        functools.partial(step_kernel, n, per),
        grid=(g_dev // per,),
        out_shape=(
            jax.ShapeDtypeStruct(weights.shape, jnp.float32),
            jax.ShapeDtypeStruct((g_dev, cells), jnp.float32),
        ),
        in_specs=[
            pl.BlockSpec(memory_space=pltpu.SMEM),
            pl.BlockSpec((span, total, cells), lambda i: (0, 0, 0)),
            pl.BlockSpec((1, total), lambda i: (0, 0)),
            pl.BlockSpec((per, cells, depth), lambda i: (i, 0, 0)),
        ],
        out_specs=(
            pl.BlockSpec((per, cells, depth), lambda i: (i, 0, 0)),
            pl.BlockSpec((g_dev, cells), lambda i: (0, 0)),
        ),
        scratch_shapes=[
            pltpu.VMEM((g_dev, total, cells), jnp.float32),
            pltpu.VMEM((per, total, depth), jnp.bfloat16),
            pltpu.VMEM((span, total, cells), jnp.bfloat16),
        ],
        compiler_params=pltpu.CompilerParams(vmem_limit_bytes=44 * 2**20),
        cost_estimate=pl.CostEstimate(
            flops=flops, bytes_accessed=6 * g_dev * cells * depth, transcendentals=0
        ),
    )(neighbours, x, times, weights)


def solution(mesh):
    return jax.shard_map(
        shards,
        mesh=mesh,
        in_specs=(
            P(("groups", "space"), None, None),
            P(("groups", "space"), None, None),
            P(("groups", "space"), None),
            P("groups"),
        ),
        out_specs=(P(("groups", "space"), None, None), P(("groups", "space"), None)),
        check_vma=False,
    )
```

```python
import functools

import jax
import jax.numpy as jnp
from jax import lax
from jax.experimental import pallas as pl
from jax.experimental.pallas import tpu as pltpu
from jax.sharding import PartitionSpec as P

HALO = 4
LIMIT = 50 * 2**20
MESH = pl.DeviceIdType.MESH


def partner(q, i, count):
    if count & (count - 1):
        return lax.rem(q + i, count), lax.rem(q + count - i, count)
    bit = 1
    out = q
    while bit <= i:
        if i & bit:
            out = out + bit * (1 - 2 * lax.rem(q // bit, 2))
        bit *= 2
    return out, out


def gather_kernel(n, snaps_hbm, w_hbm, nb_hbm, times_hbm, x, w, nb, times, snaps, wide, flat, pairs, siblings, load_sem, sems):
    rows, groups, cells = snaps.shape
    g_dev = groups // n
    span = g_dev + 2 * HALO
    chips = n // 2
    own_part = g_dev * rows
    me = lax.axis_index("space")
    q, core = me // 2, lax.rem(me, 2)
    other = 1 - core
    sibling = 2 * q + other

    load = pltpu.make_async_copy(snaps_hbm, snaps, load_sem.at[0])
    load.start()
    others = [
        pltpu.make_async_copy(a, b, load_sem.at[1 + i])
        for i, (a, b) in enumerate([(w_hbm, w), (nb_hbm, nb), (times_hbm, times)])
    ]
    barrier = pltpu.get_barrier_semaphore()
    for to in [2 * partner(q, i, chips)[0] + core for i in range(1, chips)] + [sibling]:
        pl.semaphore_signal(barrier, inc=1, device_id={"space": to}, device_id_type=MESH)
    load.wait()

    step = 16

    def relay(b):
        first = b * step
        block = snaps[:, pl.ds(first, step), :].astype(jnp.float32)
        wide[b % 2] = block.reshape(rows * step, cells)
        for p in range(step // 2):
            pair = jnp.concatenate(
                [wide[b % 2, pl.ds(2 * p + h, rows, stride=step), :] for h in range(2)], axis=0
            )
            at = (first + HALO + 2 * p) * rows
            flat[at : at + 2 * rows, :] = pair.astype(jnp.bfloat16)

    for b in range(groups // step):
        relay(b)

    edge = HALO * rows
    flat[:edge, :] = flat[groups * rows : groups * rows + edge, :]
    flat[(groups + HALO) * rows :, :] = flat[edge : 2 * edge, :]

    pl.semaphore_wait(barrier, chips)

    def chip_part(chip, length, skip=0):
        at = pl.multiple_of(chip * (2 * own_part) + skip * own_part, own_part)
        return flat.at[pl.ds(at, length * rows), :]

    def across(i):
        to = partner(q, i, chips)[0]
        return pltpu.make_async_remote_copy(
            src_ref=chip_part(to, span + g_dev),
            dst_ref=pairs.at[q],
            send_sem=sems.at[0, i],
            recv_sem=sems.at[1, i],
            device_id={"space": 2 * to + core},
            device_id_type=MESH,
        )

    def beside(i):
        source = partner(q, i, chips)[1]
        at = pl.ds(pl.multiple_of(other * own_part, own_part), span * rows)
        return pltpu.make_async_remote_copy(
            src_ref=chip_part(q, span, other) if i == 0 else pairs.at[source, at, :],
            dst_ref=siblings.at[source],
            send_sem=sems.at[2, i],
            recv_sem=sems.at[3, i],
            device_id={"space": sibling},
            device_id_type=MESH,
        )

    def place(device, block):
        at = pl.multiple_of(device * rows, rows)
        x[:, pl.ds(at, rows), :] = block.astype(jnp.float32).reshape(span, rows, cells)

    send_order = send_order_of(chips)
    wait_order = wait_order_of(chips)
    for i in send_order:
        across(i).start()
    beside(0).start()
    for other_load in others:
        other_load.start()
    place(me, chip_part(q, span, core)[...])
    for i in wait_order:
        across(i).wait_recv()
        beside(i).start()
        source = partner(q, i, chips)[1]
        at = pl.ds(pl.multiple_of(core * own_part, own_part), span * rows)
        place(2 * source + core, pairs[source, at, :])
    for i in [0] + wait_order:
        beside(i).wait_recv()
        source = partner(q, i, chips)[1] if i else q
        place(2 * source + other, siblings[source])
    for i in [0] + wait_order:
        beside(i).wait_send()
        if i:
            across(i).wait_send()
    for other_load in others:
        other_load.wait()


def send_order_of(chips):
    return list(range(chips - 1, 0, -1))


def wait_order_of(chips):
    return list(range(1, chips // 2)) + list(range(chips - 1, chips // 2 - 1, -1))


def gathered(snaps, weights, neighbours, times, n):
    rows, groups, cells = snaps.shape
    g_dev = groups // n
    span = g_dev + 2 * HALO
    chips = n // 2
    block = rows * cells
    need = (
        2 * groups * block
        + 2 * 16 * block * 4
        + 2 * (groups + 2 * HALO) * block
        + 2 * chips * (2 * span + g_dev) * block
        + 4 * span * n * block
    )
    return pl.pallas_call(
        functools.partial(gather_kernel, n),
        out_shape=[
            jax.ShapeDtypeStruct((span, rows * n, cells), jnp.float32),
            jax.ShapeDtypeStruct(weights.shape, weights.dtype),
            jax.ShapeDtypeStruct(neighbours.shape, neighbours.dtype),
            jax.ShapeDtypeStruct(times.shape, times.dtype),
        ],
        in_specs=[pl.BlockSpec(memory_space=pltpu.HBM)] * 4,
        out_specs=[pl.BlockSpec(memory_space=pltpu.VMEM)] * 4,
        scratch_shapes=[
            pltpu.VMEM(snaps.shape, jnp.bfloat16),
            pltpu.VMEM((2, rows * 16, cells), jnp.float32),
            pltpu.VMEM(((groups + 2 * HALO) * rows, cells), jnp.bfloat16),
            pltpu.VMEM((chips, (span + g_dev) * rows, cells), jnp.bfloat16),
            pltpu.VMEM((chips, span * rows, cells), jnp.bfloat16),
            pltpu.SemaphoreType.DMA((4,)),
            pltpu.SemaphoreType.DMA((4, chips)),
        ],
        compiler_params=pltpu.CompilerParams(
            collective_id=0, has_side_effects=True, vmem_limit_bytes=LIMIT
        ),
        cost_estimate=pl.CostEstimate(
            flops=0, bytes_accessed=4 * span * rows * n * cells * 20, transcendentals=0
        ),
    )(snaps, weights, neighbours, times)


def step_kernel(n, nb, x, times_in, weights, fresh_hbm, error_out, times, live, goal, inputs, xb, fresh_all, sems):
    span, total, cells = x.shape
    g_dev = span - 2 * HALO
    width = g_dev * n
    depth = weights.shape[2]
    scale = 1.0 / (depth**0.5)
    step_rate = 100.0
    me = lax.axis_index("space")
    tile = 128
    turns = total // tile

    def each(body, init):
        return body(0, init) if turns == 1 else lax.fori_loop(0, turns, body, init)

    def part_of(b):
        return pl.ds(b * tile if isinstance(b, int) else pl.multiple_of(b * tile, tile), tile)

    times[...] = times_in[...].astype(jnp.float32)
    xb[...] = x[...].astype(jnp.bfloat16)

    def rows_of(b, none):
        own = jnp.transpose(jnp.broadcast_to(times[:, part_of(b)], (tile, tile)))
        live[part_of(b), :] = (own != float(total - 1)).astype(jnp.float32)
        for g in range(0, g_dev, 2):
            def add(c, acc):
                pick = (own + 1.0 == times[:, part_of(c)]).astype(jnp.bfloat16)
                block = jnp.concatenate(
                    [xb[HALO + g + h, part_of(c), :] for h in range(2)], axis=1
                )
                return acc + jnp.dot(pick, block, preferred_element_type=jnp.float32)

            acc = each(add, jnp.zeros((tile, 2 * cells), jnp.float32))
            for h in range(2):
                goal[g + h, part_of(b), :] = acc[:, h * cells : (h + 1) * cells]
        return none

    each(rows_of, 0)

    copies = []
    for g in range(g_dev):
        for k in range(depth // cells):
            local = lax.rem(nb[g, k] - (me * g_dev + g) + HALO + width, width) + g
            inputs[g, :, k * cells : (k + 1) * cells] = xb[local]
        w = weights[g]

        def forward(b, matrix):
            out = lax.dot_general(
                inputs[g, part_of(b), :], matrix, (((1,), (1,)), ((), ())),
                preferred_element_type=jnp.float32,
            )
            return (out * scale - goal[g, part_of(b), :]) * live[part_of(b), :]

        def add_grad(b, acc):
            resid = forward(b, w).astype(jnp.bfloat16)
            return acc + lax.dot_general(
                resid, inputs[g, part_of(b), :], (((0,), (0,)), ((), ())),
                preferred_element_type=jnp.float32,
            )

        grad = each(add_grad, jnp.zeros((cells, depth), jnp.float32))
        fresh = w.astype(jnp.float32) - grad * (step_rate * 2.0 * scale / (total - 1))
        fresh_all[g] = fresh
        copies.append(pltpu.make_async_copy(fresh_all.at[g], fresh_hbm.at[g], sems.at[g]))
        copies[-1].start()
        fresh_b = fresh.astype(jnp.bfloat16)

        def add_error(b, acc):
            out = forward(b, fresh_b)
            return acc + jnp.sum(out * out, axis=0, keepdims=True)

        error = each(add_error, jnp.zeros((1, cells), jnp.float32))
        error_out[g : g + 1, :] = error * (1.0 / (total - 1))
    for copy in copies:
        copy.wait()


def shards(snapshots, weights, neighbours, time_of):
    n = lax.axis_size("space")
    g_dev, cells, depth = weights.shape
    total = time_of.shape[0]
    span = g_dev + 2 * HALO
    x, weights, neighbours, times = gathered(
        snapshots, weights, neighbours, time_of.reshape(1, total), n
    )
    flops = 6 * g_dev * total * cells * depth
    words = g_dev * cells * depth
    need = (
        6 * words
        + 2 * span * total * cells
        + 4 * (g_dev + 1) * total * cells
        + 2 * g_dev * total * depth
        + 4 * span * total * cells
    )
    return pl.pallas_call(
        functools.partial(step_kernel, n),
        out_shape=(
            jax.ShapeDtypeStruct(weights.shape, jnp.float32),
            jax.ShapeDtypeStruct((g_dev, cells), jnp.float32),
        ),
        in_specs=[
            pl.BlockSpec(memory_space=pltpu.SMEM),
            pl.BlockSpec(memory_space=pltpu.VMEM),
            pl.BlockSpec(memory_space=pltpu.VMEM),
            pl.BlockSpec(memory_space=pltpu.VMEM),
        ],
        out_specs=(
            pl.BlockSpec(memory_space=pltpu.HBM),
            pl.BlockSpec(memory_space=pltpu.VMEM),
        ),
        scratch_shapes=[
            pltpu.VMEM((1, total), jnp.float32),
            pltpu.VMEM((total, cells), jnp.float32),
            pltpu.VMEM((g_dev, total, cells), jnp.float32),
            pltpu.VMEM((g_dev, total, depth), jnp.bfloat16),
            pltpu.VMEM((span, total, cells), jnp.bfloat16),
            pltpu.VMEM((g_dev, cells, depth), jnp.float32),
            pltpu.SemaphoreType.DMA((g_dev,)),
        ],
        compiler_params=pltpu.CompilerParams(vmem_limit_bytes=need + 4 * 2**20),
        cost_estimate=pl.CostEstimate(
            flops=flops, bytes_accessed=3 * words, transcendentals=0
        ),
    )(neighbours, x, times, weights)


def solution(mesh):
    return jax.shard_map(
        shards,
        mesh=mesh,
        in_specs=(
            P(("groups", "space"), None, None),
            P(("groups", "space"), None, None),
            P(("groups", "space"), None),
            P("groups"),
        ),
        out_specs=(P(("groups", "space"), None, None), P(("groups", "space"), None)),
        check_vma=False,
    )
```

```python
import functools

import jax
import jax.numpy as jnp
from jax import lax
from jax.experimental import pallas as pl
from jax.experimental.pallas import tpu as pltpu
from jax.sharding import PartitionSpec as P

HALO = 4
LIMIT = 58 * 2**20
MESH = pl.DeviceIdType.MESH


def partner(q, i, count):
    if count & (count - 1):
        return lax.rem(q + i, count), lax.rem(q + count - i, count)
    bit = 1
    out = q
    while bit <= i:
        if i & bit:
            out = out + bit * (1 - 2 * lax.rem(q // bit, 2))
        bit *= 2
    return out, out


def gather_kernel(n, snaps_hbm, x_hbm, snaps, wide, flat, pairs, siblings, x, xb, load_sem, sems):
    rows, groups, cells = snaps.shape
    g_dev = groups // n
    span = g_dev + 2 * HALO
    chips = n // 2
    own_part = g_dev * rows
    me = lax.axis_index("space")
    q, core = me // 2, lax.rem(me, 2)
    other = 1 - core
    sibling = 2 * q + other

    load = pltpu.make_async_copy(snaps_hbm, snaps, load_sem.at[0])
    load.start()
    barrier = pltpu.get_barrier_semaphore()
    for to in [2 * partner(q, i, chips)[0] + core for i in range(1, chips)] + [sibling]:
        pl.semaphore_signal(barrier, inc=1, device_id={"space": to}, device_id_type=MESH)
    load.wait()

    step = 16

    def relay(b):
        first = b * step
        block = snaps[:, pl.ds(first, step), :].astype(jnp.float32)
        wide[b % 2] = block.reshape(rows * step, cells)
        for p in range(step // 2):
            pair = jnp.concatenate(
                [wide[b % 2, pl.ds(2 * p + h, rows, stride=step), :] for h in range(2)], axis=0
            )
            at = (first + HALO + 2 * p) * rows
            flat[at : at + 2 * rows, :] = pair.astype(jnp.bfloat16)

    for b in range(groups // step):
        relay(b)

    edge = HALO * rows
    flat[:edge, :] = flat[groups * rows : groups * rows + edge, :]
    flat[(groups + HALO) * rows :, :] = flat[edge : 2 * edge, :]

    pl.semaphore_wait(barrier, chips)

    def chip_part(chip, length, skip=0):
        at = pl.multiple_of(chip * (2 * own_part) + skip * own_part, own_part)
        return flat.at[pl.ds(at, length * rows), :]

    def across(i):
        to = partner(q, i, chips)[0]
        return pltpu.make_async_remote_copy(
            src_ref=chip_part(to, span + g_dev),
            dst_ref=pairs.at[q],
            send_sem=sems.at[0, i],
            recv_sem=sems.at[1, i],
            device_id={"space": 2 * to + core},
            device_id_type=MESH,
        )

    def beside(i):
        source = partner(q, i, chips)[1]
        at = pl.ds(pl.multiple_of(other * own_part, own_part), span * rows)
        return pltpu.make_async_remote_copy(
            src_ref=chip_part(q, span, other) if i == 0 else pairs.at[source, at, :],
            dst_ref=siblings.at[source],
            send_sem=sems.at[2, i],
            recv_sem=sems.at[3, i],
            device_id={"space": sibling},
            device_id_type=MESH,
        )

    def place(device, block):
        at = pl.multiple_of(device * rows, rows)
        x[:, pl.ds(at, rows), :] = block.astype(jnp.float32).reshape(span, rows, cells)

    send_order = send_order_of(chips)
    wait_order = wait_order_of(chips)
    for i in send_order:
        across(i).start()
    beside(0).start()
    place(me, chip_part(q, span, core)[...])
    for i in wait_order:
        across(i).wait_recv()
        beside(i).start()
        source = partner(q, i, chips)[1]
        at = pl.ds(pl.multiple_of(core * own_part, own_part), span * rows)
        place(2 * source + core, pairs[source, at, :])
    for i in [0] + wait_order:
        beside(i).wait_recv()
        source = partner(q, i, chips)[1] if i else q
        place(2 * source + other, siblings[source])
    stores = []
    for s in range(4):
        part = pl.ds(s * span // 4, span // 4)
        xb[part] = x[part].astype(jnp.bfloat16)
        stores.append(
            pltpu.make_async_copy(xb.at[part], x_hbm.at[part], load_sem.at[1 + s])
        )
        stores[-1].start()
    for i in [0] + wait_order:
        beside(i).wait_send()
        if i:
            across(i).wait_send()
    for store in stores:
        store.wait()


def send_order_of(chips):
    return list(range(chips - 1, 0, -1))


def wait_order_of(chips):
    return list(range(1, chips // 2)) + list(range(chips - 1, chips // 2 - 1, -1))


def gathered(snaps, n):
    rows, groups, cells = snaps.shape
    g_dev = groups // n
    span = g_dev + 2 * HALO
    chips = n // 2
    return pl.pallas_call(
        functools.partial(gather_kernel, n),
        out_shape=jax.ShapeDtypeStruct((span, rows * n, cells), jnp.bfloat16),
        in_specs=[pl.BlockSpec(memory_space=pltpu.HBM)],
        out_specs=pl.BlockSpec(memory_space=pltpu.HBM),
        scratch_shapes=[
            pltpu.VMEM(snaps.shape, jnp.bfloat16),
            pltpu.VMEM((2, rows * 16, cells), jnp.float32),
            pltpu.VMEM(((groups + 2 * HALO) * rows, cells), jnp.bfloat16),
            pltpu.VMEM((chips, (span + g_dev) * rows, cells), jnp.bfloat16),
            pltpu.VMEM((chips, span * rows, cells), jnp.bfloat16),
            pltpu.VMEM((span, rows * n, cells), jnp.float32),
            pltpu.VMEM((span, rows * n, cells), jnp.bfloat16),
            pltpu.SemaphoreType.DMA((5,)),
            pltpu.SemaphoreType.DMA((4, chips)),
        ],
        compiler_params=pltpu.CompilerParams(
            collective_id=0, has_side_effects=True, vmem_limit_bytes=LIMIT
        ),
        cost_estimate=pl.CostEstimate(
            flops=0, bytes_accessed=4 * span * rows * n * cells, transcendentals=0
        ),
    )(snaps)


def step_kernel(n, nb_hbm, x_hbm, times_hbm, w_hbm, fresh_hbm, error_out, nb, xb, times_in, weights, times, live, goal, inputs, resids, rounded, fresh_all, load_sem, sems):
    span, total, cells = xb.shape
    g_dev = span - 2 * HALO
    width = g_dev * n
    depth = weights.shape[2]
    scale = 1.0 / (depth**0.5)
    step_rate = 100.0
    me = lax.axis_index("space")
    tile = 128
    turns = total // tile

    loads = [
        pltpu.make_async_copy(a, b, load_sem.at[i])
        for i, (a, b) in enumerate(
            [(times_hbm, times_in), (x_hbm, xb), (nb_hbm, nb), (w_hbm, weights)]
        )
    ]
    for load in loads:
        load.start()

    def each(body, init):
        return body(0, init) if turns == 1 else lax.fori_loop(0, turns, body, init)

    def part_of(b):
        return pl.ds(b * tile if isinstance(b, int) else pl.multiple_of(b * tile, tile), tile)

    loads[0].wait()
    times[...] = times_in[...].astype(jnp.float32)
    loads[1].wait()

    def rows_of(b, none):
        own = jnp.transpose(jnp.broadcast_to(times[:, part_of(b)], (tile, tile)))
        live[part_of(b), :] = (own != float(total - 1)).astype(jnp.float32)
        for g in range(0, g_dev, 2):
            def add(c, acc):
                pick = (own + 1.0 == times[:, part_of(c)]).astype(jnp.bfloat16)
                block = jnp.concatenate(
                    [xb[HALO + g + h, part_of(c), :] for h in range(2)], axis=1
                )
                return acc + jnp.dot(pick, block, preferred_element_type=jnp.float32)

            acc = each(add, jnp.zeros((tile, 2 * cells), jnp.float32))
            for h in range(2):
                goal[g + h, part_of(b), :] = acc[:, h * cells : (h + 1) * cells]
        return none

    each(rows_of, 0)
    for load in loads[2:]:
        load.wait()

    def forward(g, b, matrix):
        out = lax.dot_general(
            inputs[g, part_of(b), :], matrix, (((1,), (1,)), ((), ())),
            preferred_element_type=jnp.float32,
        )
        return (out * scale - goal[g, part_of(b), :]) * live[part_of(b), :]

    def predict(g):
        for k in range(depth // cells):
            local = lax.rem(nb[g, k] - (me * g_dev + g) + HALO + width, width) + g
            inputs[g, :, k * cells : (k + 1) * cells] = xb[local]

        def one(b, none):
            resids[g, part_of(b), :] = forward(g, b, weights[g]).astype(jnp.bfloat16)
            return none

        each(one, 0)

    def update(g):
        def add(b, acc):
            return acc + lax.dot_general(
                resids[g, part_of(b), :], inputs[g, part_of(b), :], (((0,), (0,)), ((), ())),
                preferred_element_type=jnp.float32,
            )

        grad = each(add, jnp.zeros((cells, depth), jnp.float32))
        fresh = weights[g].astype(jnp.float32) - grad * (
            step_rate * 2.0 * scale / (total - 1)
        )
        fresh_all[g] = fresh
        rounded[g] = fresh.astype(jnp.bfloat16)

    def judge(g):
        def add(b, acc):
            out = forward(g, b, rounded[g])
            return acc + jnp.sum(out * out, axis=0, keepdims=True)

        error = each(add, jnp.zeros((1, cells), jnp.float32))
        error_out[g : g + 1, :] = error * (1.0 / (total - 1))

    copies = []
    for g in range(g_dev + 2):
        if g < g_dev:
            predict(g)
        if 1 <= g <= g_dev:
            update(g - 1)
        if g >= 2:
            judge(g - 2)
        if g >= 2 and g % 2 == 0:
            part = pl.ds(g - 2, 2)
            copies.append(
                pltpu.make_async_copy(fresh_all.at[part], fresh_hbm.at[part], sems.at[g // 2 - 1])
            )
            copies[-1].start()
    for copy in copies:
        copy.wait()


def shards(snapshots, weights, neighbours, time_of):
    n = lax.axis_size("space")
    g_dev, cells, depth = weights.shape
    total = time_of.shape[0]
    span = g_dev + 2 * HALO
    x = gathered(snapshots, n)
    words = g_dev * cells * depth
    return pl.pallas_call(
        functools.partial(step_kernel, n),
        out_shape=(
            jax.ShapeDtypeStruct(weights.shape, jnp.float32),
            jax.ShapeDtypeStruct((g_dev, cells), jnp.float32),
        ),
        in_specs=[pl.BlockSpec(memory_space=pltpu.HBM)] * 4,
        out_specs=(
            pl.BlockSpec(memory_space=pltpu.HBM),
            pl.BlockSpec(memory_space=pltpu.VMEM),
        ),
        scratch_shapes=[
            pltpu.SMEM(neighbours.shape, jnp.int32),
            pltpu.VMEM(x.shape, jnp.bfloat16),
            pltpu.VMEM((1, total), jnp.int32),
            pltpu.VMEM(weights.shape, jnp.bfloat16),
            pltpu.VMEM((1, total), jnp.float32),
            pltpu.VMEM((total, cells), jnp.float32),
            pltpu.VMEM((g_dev, total, cells), jnp.float32),
            pltpu.VMEM((g_dev, total, depth), jnp.bfloat16),
            pltpu.VMEM((g_dev, total, cells), jnp.bfloat16),
            pltpu.VMEM(weights.shape, jnp.bfloat16),
            pltpu.VMEM(weights.shape, jnp.float32),
            pltpu.SemaphoreType.DMA((4,)),
            pltpu.SemaphoreType.DMA((g_dev // 2,)),
        ],
        compiler_params=pltpu.CompilerParams(vmem_limit_bytes=LIMIT),
        cost_estimate=pl.CostEstimate(
            flops=6 * total * words, bytes_accessed=6 * words, transcendentals=0
        ),
    )(neighbours, x, time_of.reshape(1, total), weights)


def solution(mesh):
    return jax.shard_map(
        shards,
        mesh=mesh,
        in_specs=(
            P(("groups", "space"), None, None),
            P(("groups", "space"), None, None),
            P(("groups", "space"), None),
            P("groups"),
        ),
        out_specs=(P(("groups", "space"), None, None), P(("groups", "space"), None)),
        check_vma=False,
    )
```

```python
import functools

import jax
import jax.numpy as jnp
from jax import lax
from jax.experimental import pallas as pl
from jax.experimental.pallas import tpu as pltpu
from jax.sharding import PartitionSpec as P

HALO = 4
LIMIT = 58 * 2**20
MESH = pl.DeviceIdType.MESH


def partner(q, i, count):
    if count & (count - 1):
        return lax.rem(q + i, count), lax.rem(q + count - i, count)
    bit = 1
    out = q
    while bit <= i:
        if i & bit:
            out = out + bit * (1 - 2 * lax.rem(q // bit, 2))
        bit *= 2
    return out, out


def gather_kernel(n, snaps_hbm, x_hbm, snaps, wide, flat, pairs, siblings, x, xb, load_sem, store_sem, sems):
    rows, groups, cells = snaps.shape
    g_dev = groups // n
    span = g_dev + 2 * HALO
    chips = n // 2
    own_part = g_dev * rows
    me = lax.axis_index("space")
    q, core = me // 2, lax.rem(me, 2)
    other = 1 - core
    sibling = 2 * q + other

    load = pltpu.make_async_copy(snaps_hbm, snaps, load_sem)
    load.start()
    barrier = pltpu.get_barrier_semaphore()
    for to in [2 * partner(q, i, chips)[0] + core for i in range(1, chips)] + [sibling]:
        pl.semaphore_signal(barrier, inc=1, device_id={"space": to}, device_id_type=MESH)
    load.wait()

    step = 16

    def relay(b):
        first = b * step
        block = snaps[:, pl.ds(first, step), :].astype(jnp.float32)
        wide[b % 2] = block.reshape(rows * step, cells)
        for p in range(step // 2):
            pair = jnp.concatenate(
                [wide[b % 2, pl.ds(2 * p + h, rows, stride=step), :] for h in range(2)], axis=0
            )
            at = (first + HALO + 2 * p) * rows
            flat[at : at + 2 * rows, :] = pair.astype(jnp.bfloat16)

    for b in range(groups // step):
        relay(b)

    edge = HALO * rows
    flat[:edge, :] = flat[groups * rows : groups * rows + edge, :]
    flat[(groups + HALO) * rows :, :] = flat[edge : 2 * edge, :]

    pl.semaphore_wait(barrier, chips)

    def chip_part(chip, length, skip=0):
        at = pl.multiple_of(chip * (2 * own_part) + skip * own_part, own_part)
        return flat.at[pl.ds(at, length * rows), :]

    def across(i):
        to = partner(q, i, chips)[0]
        return pltpu.make_async_remote_copy(
            src_ref=chip_part(to, span + g_dev),
            dst_ref=pairs.at[q],
            send_sem=sems.at[0, i],
            recv_sem=sems.at[1, i],
            device_id={"space": 2 * to + core},
            device_id_type=MESH,
        )

    def beside(i):
        source = partner(q, i, chips)[1]
        at = pl.ds(pl.multiple_of(other * own_part, own_part), span * rows)
        return pltpu.make_async_remote_copy(
            src_ref=chip_part(q, span, other) if i == 0 else pairs.at[source, at, :],
            dst_ref=siblings.at[source],
            send_sem=sems.at[2, i],
            recv_sem=sems.at[3, i],
            device_id={"space": sibling},
            device_id_type=MESH,
        )

    def place(device, block):
        at = pl.multiple_of(device * rows, rows)
        x[:, pl.ds(at, rows), :] = block.astype(jnp.float32).reshape(span, rows, cells)

    send_order = send_order_of(chips)
    wait_order = wait_order_of(chips)
    for i in send_order:
        across(i).start()
    beside(0).start()
    place(me, chip_part(q, span, core)[...])
    stores = []

    def finish(i):
        beside(i).wait_recv()
        source = partner(q, i, chips)[1] if i else q
        place(2 * source + other, siblings[source])
        part = pl.ds(pl.multiple_of(source * 2 * rows, 2 * rows), 2 * rows)
        xb[:, part, :] = x[:, part, :].astype(jnp.bfloat16)
        stores.append(
            pltpu.make_async_copy(xb.at[:, part, :], x_hbm.at[:, part, :], store_sem.at[i])
        )
        stores[-1].start()

    for done, i in enumerate(wait_order):
        across(i).wait_recv()
        beside(i).start()
        source = partner(q, i, chips)[1]
        at = pl.ds(pl.multiple_of(core * own_part, own_part), span * rows)
        place(2 * source + core, pairs[source, at, :])
        if done >= 2:
            finish(([0] + wait_order)[done - 2])
    for i in ([0] + wait_order)[max(chips - 3, 0):]:
        finish(i)
    for i in [0] + wait_order:
        beside(i).wait_send()
        if i:
            across(i).wait_send()
    for store in stores:
        store.wait()


def send_order_of(chips):
    return list(range(chips - 1, 0, -1))


def wait_order_of(chips):
    return list(range(1, chips // 2)) + list(range(chips - 1, chips // 2 - 1, -1))


def gathered(snaps, n):
    rows, groups, cells = snaps.shape
    g_dev = groups // n
    span = g_dev + 2 * HALO
    chips = n // 2
    return pl.pallas_call(
        functools.partial(gather_kernel, n),
        out_shape=jax.ShapeDtypeStruct((span, rows * n, cells), jnp.bfloat16),
        in_specs=[pl.BlockSpec(memory_space=pltpu.HBM)],
        out_specs=pl.BlockSpec(memory_space=pltpu.HBM),
        scratch_shapes=[
            pltpu.VMEM(snaps.shape, jnp.bfloat16),
            pltpu.VMEM((2, rows * 16, cells), jnp.float32),
            pltpu.VMEM(((groups + 2 * HALO) * rows, cells), jnp.bfloat16),
            pltpu.VMEM((chips, (span + g_dev) * rows, cells), jnp.bfloat16),
            pltpu.VMEM((chips, span * rows, cells), jnp.bfloat16),
            pltpu.VMEM((span, rows * n, cells), jnp.float32),
            pltpu.VMEM((span, rows * n, cells), jnp.bfloat16),
            pltpu.SemaphoreType.DMA,
            pltpu.SemaphoreType.DMA((chips,)),
            pltpu.SemaphoreType.DMA((4, chips)),
        ],
        compiler_params=pltpu.CompilerParams(
            collective_id=0, has_side_effects=True, vmem_limit_bytes=LIMIT
        ),
        cost_estimate=pl.CostEstimate(
            flops=0, bytes_accessed=4 * span * rows * n * cells, transcendentals=0
        ),
    )(snaps)


def step_kernel(n, nb_hbm, x_hbm, times_hbm, w_hbm, fresh_hbm, error_out, nb, xb, times_in, weights, times, live, goal, inputs, resids, rounded, fresh_all, load_sem, sems):
    span, total, cells = xb.shape
    g_dev = span - 2 * HALO
    width = g_dev * n
    depth = weights.shape[2]
    scale = 1.0 / (depth**0.5)
    step_rate = 100.0
    me = lax.axis_index("space")
    tile = 128
    turns = total // tile

    loads = [
        pltpu.make_async_copy(a, b, load_sem.at[i])
        for i, (a, b) in enumerate(
            [(times_hbm, times_in), (x_hbm, xb), (nb_hbm, nb)]
            + [(w_hbm.at[g], weights.at[g]) for g in range(g_dev)]
        )
    ]
    for load in loads:
        load.start()

    def each(body, init):
        return body(0, init) if turns == 1 else lax.fori_loop(0, turns, body, init)

    def part_of(b):
        return pl.ds(b * tile if isinstance(b, int) else pl.multiple_of(b * tile, tile), tile)

    loads[0].wait()
    times[...] = times_in[...].astype(jnp.float32)
    loads[1].wait()

    def rows_of(b, none):
        own = jnp.transpose(jnp.broadcast_to(times[:, part_of(b)], (tile, tile)))
        live[part_of(b), :] = (own != float(total - 1)).astype(jnp.float32)
        for g in range(0, g_dev, 2):
            def add(c, acc):
                pick = (own + 1.0 == times[:, part_of(c)]).astype(jnp.bfloat16)
                block = jnp.concatenate(
                    [xb[HALO + g + h, part_of(c), :] for h in range(2)], axis=1
                )
                return acc + jnp.dot(pick, block, preferred_element_type=jnp.float32)

            acc = each(add, jnp.zeros((tile, 2 * cells), jnp.float32))
            for h in range(2):
                goal[g + h, part_of(b), :] = acc[:, h * cells : (h + 1) * cells]
        return none

    each(rows_of, 0)
    loads[2].wait()

    def forward(g, b, matrix):
        out = lax.dot_general(
            inputs[g, part_of(b), :], matrix, (((1,), (1,)), ((), ())),
            preferred_element_type=jnp.float32,
        )
        return (out * scale - goal[g, part_of(b), :]) * live[part_of(b), :]

    def predict(g):
        for k in range(depth // cells):
            local = lax.rem(nb[g, k] - (me * g_dev + g) + HALO + width, width) + g
            inputs[g, :, k * cells : (k + 1) * cells] = xb[local]

        def one(b, none):
            resids[g, part_of(b), :] = forward(g, b, weights[g]).astype(jnp.bfloat16)
            return none

        each(one, 0)

    def update(g):
        def add(b, acc):
            return acc + lax.dot_general(
                resids[g, part_of(b), :], inputs[g, part_of(b), :], (((0,), (0,)), ((), ())),
                preferred_element_type=jnp.float32,
            )

        grad = each(add, jnp.zeros((cells, depth), jnp.float32))
        fresh = weights[g].astype(jnp.float32) - grad * (
            step_rate * 2.0 * scale / (total - 1)
        )
        fresh_all[g] = fresh
        rounded[g] = fresh.astype(jnp.bfloat16)

    def judge(g):
        def add(b, acc):
            out = forward(g, b, rounded[g])
            return acc + jnp.sum(out * out, axis=0, keepdims=True)

        error = each(add, jnp.zeros((1, cells), jnp.float32))
        error_out[g : g + 1, :] = error * (1.0 / (total - 1))

    copies = []

    def send(first, count):
        part = pl.ds(first, count)
        copies.append(
            pltpu.make_async_copy(fresh_all.at[part], fresh_hbm.at[part], sems.at[first])
        )
        copies[-1].start()

    for g in range(g_dev + 2):
        if g < g_dev and g % 4 == 0:
            for load in loads[3 + g : 3 + g + 4]:
                load.wait()
        if g < g_dev:
            predict(g)
        if 1 <= g <= g_dev:
            update(g - 1)
        if g >= 2:
            judge(g - 2)
        if 1 <= g <= g_dev and g % 2 == 0:
            send(g - 2, 2)
    for copy in copies:
        copy.wait()


def shards(snapshots, weights, neighbours, time_of):
    n = lax.axis_size("space")
    g_dev, cells, depth = weights.shape
    total = time_of.shape[0]
    span = g_dev + 2 * HALO
    x = gathered(snapshots, n)
    words = g_dev * cells * depth
    return pl.pallas_call(
        functools.partial(step_kernel, n),
        out_shape=(
            jax.ShapeDtypeStruct(weights.shape, jnp.float32),
            jax.ShapeDtypeStruct((g_dev, cells), jnp.float32),
        ),
        in_specs=[pl.BlockSpec(memory_space=pltpu.HBM)] * 4,
        out_specs=(
            pl.BlockSpec(memory_space=pltpu.HBM),
            pl.BlockSpec(memory_space=pltpu.VMEM),
        ),
        scratch_shapes=[
            pltpu.SMEM(neighbours.shape, jnp.int32),
            pltpu.VMEM(x.shape, jnp.bfloat16),
            pltpu.VMEM((1, total), jnp.int32),
            pltpu.VMEM(weights.shape, jnp.bfloat16),
            pltpu.VMEM((1, total), jnp.float32),
            pltpu.VMEM((total, cells), jnp.float32),
            pltpu.VMEM((g_dev, total, cells), jnp.float32),
            pltpu.VMEM((g_dev, total, depth), jnp.bfloat16),
            pltpu.VMEM((g_dev, total, cells), jnp.bfloat16),
            pltpu.VMEM(weights.shape, jnp.bfloat16),
            pltpu.VMEM(weights.shape, jnp.float32),
            pltpu.SemaphoreType.DMA((3 + g_dev,)),
            pltpu.SemaphoreType.DMA((g_dev,)),
        ],
        compiler_params=pltpu.CompilerParams(vmem_limit_bytes=LIMIT),
        cost_estimate=pl.CostEstimate(
            flops=6 * total * words, bytes_accessed=6 * words, transcendentals=0
        ),
    )(neighbours, x, time_of.reshape(1, total), weights)


def solution(mesh):
    return jax.shard_map(
        shards,
        mesh=mesh,
        in_specs=(
            P(("groups", "space"), None, None),
            P(("groups", "space"), None, None),
            P(("groups", "space"), None),
            P("groups"),
        ),
        out_specs=(P(("groups", "space"), None, None), P(("groups", "space"), None)),
        check_vma=False,
    )
```

```python
import functools

import jax
import jax.numpy as jnp
from jax import lax
from jax.experimental import pallas as pl
from jax.experimental.pallas import tpu as pltpu
from jax.sharding import PartitionSpec as P

HALO = 4
LIMIT = 58 * 2**20
MESH = pl.DeviceIdType.MESH


def partner(q, i, count):
    if count & (count - 1):
        return lax.rem(q + i, count), lax.rem(q + count - i, count)
    bit = 1
    out = q
    while bit <= i:
        if i & bit:
            out = out + bit * (1 - 2 * lax.rem(q // bit, 2))
        bit *= 2
    return out, out


def gather_kernel(n, snaps_hbm, x_hbm, snaps, wide, flat, pairs, siblings, x, xb, load_sem, store_sem, sems):
    rows, groups, cells = snaps.shape
    g_dev = groups // n
    span = g_dev + 2 * HALO
    chips = n // 2
    own_part = g_dev * rows
    me = lax.axis_index("space")
    q, core = me // 2, lax.rem(me, 2)
    other = 1 - core
    sibling = 2 * q + other

    load = pltpu.make_async_copy(snaps_hbm, snaps, load_sem)
    load.start()
    barrier = pltpu.get_barrier_semaphore()
    for to in [2 * partner(q, i, chips)[0] + core for i in range(1, chips)] + [sibling]:
        pl.semaphore_signal(barrier, inc=1, device_id={"space": to}, device_id_type=MESH)
    load.wait()

    step = 16

    def relay(b):
        first = b * step
        block = snaps[:, pl.ds(first, step), :].astype(jnp.float32)
        wide[b % 2] = block.reshape(rows * step, cells)
        for p in range(step // 2):
            pair = jnp.concatenate(
                [wide[b % 2, pl.ds(2 * p + h, rows, stride=step), :] for h in range(2)], axis=0
            )
            at = (first + HALO + 2 * p) * rows
            flat[at : at + 2 * rows, :] = pair.astype(jnp.bfloat16)

    for b in range(groups // step):
        relay(b)

    edge = HALO * rows
    flat[:edge, :] = flat[groups * rows : groups * rows + edge, :]
    flat[(groups + HALO) * rows :, :] = flat[edge : 2 * edge, :]

    pl.semaphore_wait(barrier, chips)

    def chip_part(chip, length, skip=0):
        at = pl.multiple_of(chip * (2 * own_part) + skip * own_part, own_part)
        return flat.at[pl.ds(at, length * rows), :]

    def across(i):
        to = partner(q, i, chips)[0]
        return pltpu.make_async_remote_copy(
            src_ref=chip_part(to, span + g_dev),
            dst_ref=pairs.at[q],
            send_sem=sems.at[0, i],
            recv_sem=sems.at[1, i],
            device_id={"space": 2 * to + core},
            device_id_type=MESH,
        )

    def beside(i):
        source = partner(q, i, chips)[1]
        at = pl.ds(pl.multiple_of(other * own_part, own_part), span * rows)
        return pltpu.make_async_remote_copy(
            src_ref=chip_part(q, span, other) if i == 0 else pairs.at[source, at, :],
            dst_ref=siblings.at[source],
            send_sem=sems.at[2, i],
            recv_sem=sems.at[3, i],
            device_id={"space": sibling},
            device_id_type=MESH,
        )

    def place(device, block):
        at = pl.multiple_of(device * rows, rows)
        x[:, pl.ds(at, rows), :] = block.astype(jnp.float32).reshape(span, rows, cells)

    send_order = send_order_of(chips)
    wait_order = wait_order_of(chips)
    for i in send_order:
        across(i).start()
    beside(0).start()
    place(me, chip_part(q, span, core)[...])
    stores = []

    def finish(i):
        beside(i).wait_recv()
        source = partner(q, i, chips)[1] if i else q
        place(2 * source + other, siblings[source])
        part = pl.ds(pl.multiple_of(source * 2 * rows, 2 * rows), 2 * rows)
        xb[:, part, :] = x[:, part, :].astype(jnp.bfloat16)
        stores.append(
            pltpu.make_async_copy(xb.at[:, part, :], x_hbm.at[:, part, :], store_sem.at[i])
        )
        stores[-1].start()

    for i in wait_order:
        across(i).wait_recv()
        beside(i).start()
        source = partner(q, i, chips)[1]
        at = pl.ds(pl.multiple_of(core * own_part, own_part), span * rows)
        place(2 * source + core, pairs[source, at, :])
    for i in [0] + wait_order:
        finish(i)
    for i in [0] + wait_order:
        beside(i).wait_send()
        if i:
            across(i).wait_send()
    for store in stores:
        store.wait()


def send_order_of(chips):
    return list(range(1, chips))


def wait_order_of(chips):
    return list(range(1, chips // 2)) + list(range(chips - 1, chips // 2 - 1, -1))


def gathered(snaps, n):
    rows, groups, cells = snaps.shape
    g_dev = groups // n
    span = g_dev + 2 * HALO
    chips = n // 2
    return pl.pallas_call(
        functools.partial(gather_kernel, n),
        out_shape=jax.ShapeDtypeStruct((span, rows * n, cells), jnp.bfloat16),
        in_specs=[pl.BlockSpec(memory_space=pltpu.HBM)],
        out_specs=pl.BlockSpec(memory_space=pltpu.HBM),
        scratch_shapes=[
            pltpu.VMEM(snaps.shape, jnp.bfloat16),
            pltpu.VMEM((2, rows * 16, cells), jnp.float32),
            pltpu.VMEM(((groups + 2 * HALO) * rows, cells), jnp.bfloat16),
            pltpu.VMEM((chips, (span + g_dev) * rows, cells), jnp.bfloat16),
            pltpu.VMEM((chips, span * rows, cells), jnp.bfloat16),
            pltpu.VMEM((span, rows * n, cells), jnp.float32),
            pltpu.VMEM((span, rows * n, cells), jnp.bfloat16),
            pltpu.SemaphoreType.DMA,
            pltpu.SemaphoreType.DMA((chips,)),
            pltpu.SemaphoreType.DMA((4, chips)),
        ],
        compiler_params=pltpu.CompilerParams(
            collective_id=0, has_side_effects=True, vmem_limit_bytes=LIMIT
        ),
        cost_estimate=pl.CostEstimate(
            flops=0, bytes_accessed=4 * span * rows * n * cells, transcendentals=0
        ),
    )(snaps)


def step_kernel(n, nb_hbm, x_hbm, times_hbm, w_hbm, fresh_hbm, error_out, nb, xb, times_in, weights, times, live, goal, inputs, resids, rounded, fresh_all, load_sem, sems):
    span, total, cells = xb.shape
    g_dev = span - 2 * HALO
    width = g_dev * n
    depth = weights.shape[2]
    scale = 1.0 / (depth**0.5)
    step_rate = 100.0
    me = lax.axis_index("space")
    tile = 128
    turns = total // tile

    loads = [
        pltpu.make_async_copy(a, b, load_sem.at[i])
        for i, (a, b) in enumerate(
            [(times_hbm, times_in), (x_hbm, xb), (nb_hbm, nb)]
            + [(w_hbm.at[g], weights.at[g]) for g in range(g_dev)]
        )
    ]
    for load in loads:
        load.start()

    def each(body, init):
        return body(0, init) if turns == 1 else lax.fori_loop(0, turns, body, init)

    def part_of(b):
        return pl.ds(b * tile if isinstance(b, int) else pl.multiple_of(b * tile, tile), tile)

    loads[0].wait()
    times[...] = times_in[...].astype(jnp.float32)
    loads[1].wait()

    def rows_of(b, none):
        own = jnp.transpose(jnp.broadcast_to(times[:, part_of(b)], (tile, tile)))
        live[part_of(b), :] = (own != float(total - 1)).astype(jnp.float32)
        for g in range(0, g_dev, 2):
            def add(c, acc):
                pick = (own + 1.0 == times[:, part_of(c)]).astype(jnp.bfloat16)
                block = jnp.concatenate(
                    [xb[HALO + g + h, part_of(c), :] for h in range(2)], axis=1
                )
                return acc + jnp.dot(pick, block, preferred_element_type=jnp.float32)

            acc = each(add, jnp.zeros((tile, 2 * cells), jnp.float32))
            for h in range(2):
                goal[g + h, part_of(b), :] = acc[:, h * cells : (h + 1) * cells]
        return none

    each(rows_of, 0)
    loads[2].wait()

    def forward(g, b, matrix):
        out = lax.dot_general(
            inputs[g, part_of(b), :], matrix, (((1,), (1,)), ((), ())),
            preferred_element_type=jnp.float32,
        )
        return (out * scale - goal[g, part_of(b), :]) * live[part_of(b), :]

    def predict(g):
        for k in range(depth // cells):
            local = lax.rem(nb[g, k] - (me * g_dev + g) + HALO + width, width) + g
            inputs[g, :, k * cells : (k + 1) * cells] = xb[local]

        def one(b, none):
            resids[g, part_of(b), :] = forward(g, b, weights[g]).astype(jnp.bfloat16)
            return none

        each(one, 0)

    def update(g):
        def add(b, acc):
            return acc + lax.dot_general(
                resids[g, part_of(b), :], inputs[g, part_of(b), :], (((0,), (0,)), ((), ())),
                preferred_element_type=jnp.float32,
            )

        grad = each(add, jnp.zeros((cells, depth), jnp.float32))
        fresh = weights[g].astype(jnp.float32) - grad * (
            step_rate * 2.0 * scale / (total - 1)
        )
        fresh_all[g] = fresh
        rounded[g] = fresh.astype(jnp.bfloat16)

    def judge(g):
        def add(b, acc):
            out = forward(g, b, rounded[g])
            return acc + jnp.sum(out * out, axis=0, keepdims=True)

        error = each(add, jnp.zeros((1, cells), jnp.float32))
        error_out[g : g + 1, :] = error * (1.0 / (total - 1))

    copies = []

    def send(first, count):
        part = pl.ds(first, count)
        copies.append(
            pltpu.make_async_copy(fresh_all.at[part], fresh_hbm.at[part], sems.at[first])
        )
        copies[-1].start()

    for g in range(g_dev + 2):
        if g < g_dev and g % 4 == 0:
            for load in loads[3 + g : 3 + g + 4]:
                load.wait()
        if g < g_dev:
            predict(g)
        if 1 <= g <= g_dev:
            update(g - 1)
        if g >= 2:
            judge(g - 2)
        if 1 <= g <= g_dev and g % 2 == 0:
            send(g - 2, 2)
    for copy in copies:
        copy.wait()


def shards(snapshots, weights, neighbours, time_of):
    n = lax.axis_size("space")
    g_dev, cells, depth = weights.shape
    total = time_of.shape[0]
    span = g_dev + 2 * HALO
    x = gathered(snapshots, n)
    words = g_dev * cells * depth
    return pl.pallas_call(
        functools.partial(step_kernel, n),
        out_shape=(
            jax.ShapeDtypeStruct(weights.shape, jnp.float32),
            jax.ShapeDtypeStruct((g_dev, cells), jnp.float32),
        ),
        in_specs=[pl.BlockSpec(memory_space=pltpu.HBM)] * 4,
        out_specs=(
            pl.BlockSpec(memory_space=pltpu.HBM),
            pl.BlockSpec(memory_space=pltpu.VMEM),
        ),
        scratch_shapes=[
            pltpu.SMEM(neighbours.shape, jnp.int32),
            pltpu.VMEM(x.shape, jnp.bfloat16),
            pltpu.VMEM((1, total), jnp.int32),
            pltpu.VMEM(weights.shape, jnp.bfloat16),
            pltpu.VMEM((1, total), jnp.float32),
            pltpu.VMEM((total, cells), jnp.float32),
            pltpu.VMEM((g_dev, total, cells), jnp.float32),
            pltpu.VMEM((g_dev, total, depth), jnp.bfloat16),
            pltpu.VMEM((g_dev, total, cells), jnp.bfloat16),
            pltpu.VMEM(weights.shape, jnp.bfloat16),
            pltpu.VMEM(weights.shape, jnp.float32),
            pltpu.SemaphoreType.DMA((3 + g_dev,)),
            pltpu.SemaphoreType.DMA((g_dev,)),
        ],
        compiler_params=pltpu.CompilerParams(vmem_limit_bytes=LIMIT),
        cost_estimate=pl.CostEstimate(
            flops=6 * total * words, bytes_accessed=6 * words, transcendentals=0
        ),
    )(neighbours, x, time_of.reshape(1, total), weights)


def solution(mesh):
    return jax.shard_map(
        shards,
        mesh=mesh,
        in_specs=(
            P(("groups", "space"), None, None),
            P(("groups", "space"), None, None),
            P(("groups", "space"), None),
            P("groups"),
        ),
        out_specs=(P(("groups", "space"), None, None), P(("groups", "space"), None)),
        check_vma=False,
    )
```
